768 devices in a mesh: ri: 32 (over x, y), ao: 24 (over z, core).
Axes of the slice: x: 4, y: 8, z: 12, core: 2. Of those that a mesh axis runs over, the one named last changes fastest.
Arguments:
- three_centre: bfloat16 [768, 1152, 768], P('ri', 'ao'), may hold values from -6 to 6
- x_mask: int32 [32, 144, 32], P('ri', 'ao'), may hold values 0 or 1
- occ_green: bfloat16 [768, 768], P('ao'), may hold values from -0.21875 to 0.21875
- virt_green: bfloat16 [768, 768], P('ao'), may hold values from -0.21875 to 0.21875
- green_mask: int32 [2, 32, 32], replicated, may hold values 0 or 1
- nu_blocks: int32 [32], replicated, may hold values from 0 to 31, each once
Outputs:
- contracted: bfloat16 [1152, 768, 768], P('ao', 'ri')
The draws below stay inside these ranges and needn't reach their ends.
Inputs may be any that keep to these rules, and one draw needn't show every extreme that they name: `nu_blocks`: a permutation of the 32 AO blocks.
All inputs are finite; a program needn't handle non-finite values. No bound on the sum of `x_mask` on one device may be relied on, other than what follows from the above.
Results may differ from the reference program's by a relative error of at most 0.0049.
Values may be sent and summed in bfloat16 or wider, within the bound.
No kernel may reach another device: no remote copies, remote signals or barrier semaphores. Data moves between devices by JAX's collectives and lax.ppermute only.
A program may use at most 64 MiB of HBM per device.

```python
import jax
import jax.numpy as jnp
from jax import lax

B = 24
RB = 8
NB = 32
NAO = 768
RI = 1152


def touch_ends(entries, stream_key, least, top_value):
    place = [jax.random.randint(jax.random.fold_in(stream_key, axis), (), 0, length) for axis, length in enumerate(entries.shape)]
    main_axis = entries.shape.index(max(entries.shape))
    beside = place[:main_axis] + [(place[main_axis] + 1) % entries.shape[main_axis]] + place[main_axis + 1:]
    return entries.at[tuple(place)].set(least).at[tuple(beside)].set(top_value)


def level_of(rng, extent, shards, low, largest):
    def one(axis_at, shards_of):
        steps = jax.random.uniform(jax.random.fold_in(jax.random.fold_in(rng, 6), axis_at), (shards_of,), jnp.float32, low / len(shards), largest / len(shards))
        return jnp.repeat(jnp.exp(steps), extent[axis_at] // shards_of).reshape((-1,) + (1,) * (len(extent) - axis_at - 1))

    factor_of = one(*shards[0])
    for cut in shards[1:]:
        factor_of = factor_of * one(*cut)
    return factor_of


def normal_values(rng, dims, scale, most, shards=(), held_as=jnp.bfloat16):
    drawn = scale * jax.random.normal(rng, dims, jnp.float32)
    if shards:
        drawn = drawn * level_of(rng, dims, shards, -0.22, 0.18)
    return jnp.clip(drawn, -most, most).astype(held_as)


def setup_inputs(seed: int = 0) -> dict:
    keys = jax.random.split(jax.random.key(seed), 7)
    return {
        "three_centre": normal_values(keys[0], (NAO, RI, NAO), 1.0, 6.0, ((0, 32), (1, 24))),
        "x_mask": touch_ends((jax.random.randint(keys[1], (NB, RI // RB, NB), 0, 4) < 3).astype(jnp.int32), jax.random.fold_in(keys[1], 1), 0, 1),
        "occ_green": normal_values(keys[2], (NAO, NAO), NAO ** -0.5, 0.21875, ((0, 24),)),
        "virt_green": normal_values(keys[3], (NAO, NAO), NAO ** -0.5, 0.21875, ((0, 24),)),
        "green_mask": touch_ends((jax.random.randint(keys[4], (2, NB, NB), 0, 4) < 3).astype(jnp.int32), jax.random.fold_in(keys[4], 1), 0, 1),
        "nu_blocks": jax.random.permutation(keys[5], NB).astype(jnp.int32),
    }


def expand_green(matrix, block_table):
    widened = jnp.broadcast_to(block_table[:, None, :, None], (NB, B, NB, B)).reshape(NAO, NAO)
    return matrix * widened.astype(matrix.dtype)


def reference(three_centre, x_mask, occ_green, virt_green, green_mask, nu_blocks):
    occ_masked = expand_green(occ_green, green_mask[0])
    virt_masked = expand_green(virt_green, green_mask[1])
    virt_rows = virt_masked.reshape(NB, B, NAO)[nu_blocks].reshape(NAO, NAO)
    occ_wide = occ_masked.astype(jnp.float32)
    virt_wide = virt_rows.astype(jnp.float32)

    def one_slab(offset):
        window = lax.dynamic_slice_in_dim(three_centre, offset, RB, 1)
        mask_slice = lax.dynamic_slice_in_dim(x_mask, offset // RB, 1, 1)[:, 0, :]
        shaped = window.reshape(NB, B, RB, NB, B)
        masked = (shaped * mask_slice[:, None, None, :, None].astype(jnp.bfloat16)).reshape(NAO, RB, NAO)
        half_step = jnp.einsum("rpm,ml->rpl", masked.astype(jnp.float32), occ_wide,
                               precision=lax.Precision.HIGHEST).astype(jnp.bfloat16)
        result = jnp.einsum("rpl,rq->plq", half_step.astype(jnp.float32), virt_wide,
                            precision=lax.Precision.HIGHEST)
        return result.astype(jnp.bfloat16)

    starts = jnp.arange(RI // RB, dtype=jnp.int32) * RB
    all_slabs = lax.map(one_slab, starts)
    return all_slabs.reshape(RI, NAO, NAO)
```

```python
import functools

import jax
import jax.numpy as jnp
from jax import lax
from jax.experimental import pallas as pl
from jax.experimental.pallas import tpu as pltpu
from jax.sharding import PartitionSpec as P

LANES = 128
SUB = 8
GROUP = LANES // SUB
PANEL = 32


def exchange(parts):
    shape = parts[0].shape
    lane_group = lax.broadcasted_iota(jnp.int32, shape, 1) // SUB
    now = [pltpu.roll(part, SUB * p, 1) if p else part for p, part in enumerate(parts)]
    now = [now[(-k) % GROUP] for k in range(GROUP)]
    for bit in (1, 2, 4, 8):
        taken = (lane_group & bit) != 0
        now = [jnp.where(taken, now[(k - bit) % GROUP], now[k]) for k in range(GROUP)]
    return now


def half_kernel(core_ref, x_ref, kept_ref, own_ref, other_ref, out_ref, occ_ref, half_ref):
    rows, slab, width = x_ref.shape

    @pl.when(pl.program_id(0) == 0)
    def _():
        core = core_ref[0]
        for panel in range(own_ref.shape[0] // PANEL):
            here = pl.ds(panel * PANEL, PANEL)
            for ref, place in ((own_ref, core), (other_ref, 1 - core)):
                first = pl.multiple_of((2 * panel + place) * PANEL, PANEL)
                occ_ref[pl.ds(first, PANEL), :] = ref[here, :]

    local_cols = width // out_ref.shape[0]
    kept = kept_ref[0].astype(jnp.float32).astype(jnp.bfloat16)
    block_count = kept.shape[1]
    block = lax.broadcasted_iota(jnp.int32, (block_count, width), 0)
    column = lax.broadcasted_iota(jnp.int32, (block_count, width), 1)
    first = block * (width // block_count)
    spread = ((column >= first) & (column < first + width // block_count)).astype(jnp.float32).astype(jnp.bfloat16)
    wide = jnp.dot(kept, spread, preferred_element_type=jnp.float32)
    ri_rows = slab // kept.shape[0]
    wide = jnp.concatenate(
        [jnp.broadcast_to(wide[i : i + 1], (ri_rows, width)) for i in range(kept.shape[0])], 0
    ).astype(jnp.bfloat16)
    masked = (x_ref[...] * wide[None]).reshape(rows * slab, width)
    highs = out_ref.shape[0] // GROUP
    for third in range(local_cols // SUB):
        columns = pl.ds(third * highs * LANES, highs * LANES)
        half = jnp.dot(masked, occ_ref[:, columns], preferred_element_type=jnp.float32)
        for high in range(highs):
            half_ref[third * highs + high] = half[:, high * LANES : (high + 1) * LANES]
    for third in range(local_cols // SUB):
        for high in range(highs):
            plane = half_ref.at[third * highs + high]
            parts = [plane[pl.ds(p, rows, stride=slab), :] for p in range(slab)]
            for low, part in enumerate(exchange(parts)):
                out_ref[high * GROUP + low, :, pl.ds(third * LANES, LANES)] = part.astype(jnp.bfloat16)


def last_kernel(turn_ref, sent_ref, virt_ref, out_ref, sum_ref):
    slab, local_cols, width = out_ref.shape
    sum_ref[...] = lax.dot_general(
        sent_ref[...], virt_ref[...], (((0,), (0,)), ((), ())), preferred_element_type=jnp.float32
    )
    turn = turn_ref[0]
    for p in range(slab):
        place = lax.rem(p + turn, GROUP)
        pieces = [
            sum_ref[pl.ds(pl.multiple_of(third * LANES + place * SUB, SUB), SUB), :]
            for third in range(local_cols // SUB)
        ]
        out_ref[p] = jnp.concatenate(pieces, 0).astype(jnp.bfloat16)


def half_contract(core, three_centre, x_mask, own, other, groups):
    rows, slab, width = three_centre.shape
    chunks = slab // GROUP
    lanes = width // groups * GROUP
    kept = x_mask.reshape(chunks, -1, x_mask.shape[-1])
    return pl.pallas_call(
        half_kernel,
        grid=(chunks,),
        in_specs=[
            pl.BlockSpec(memory_space=pltpu.SMEM),
            pl.BlockSpec((rows, GROUP, width), lambda c: (0, c, 0)),
            pl.BlockSpec((1,) + kept.shape[1:], lambda c: (c, 0, 0)),
            pl.BlockSpec(own.shape, lambda c: (0, 0)),
            pl.BlockSpec(other.shape, lambda c: (0, 0)),
        ],
        out_specs=pl.BlockSpec((groups, rows, lanes), lambda c: (0, 0, c)),
        out_shape=jax.ShapeDtypeStruct((groups, rows, chunks * lanes), jnp.bfloat16),
        scratch_shapes=[
            pltpu.VMEM((width, width), jnp.bfloat16),
            pltpu.VMEM((width // LANES, rows * GROUP, LANES), jnp.float32),
        ],
        compiler_params=pltpu.CompilerParams(vmem_limit_bytes=60 * 2**20),
        name="half_contract",
    )(core, three_centre, kept, own, other)


def last_contract(sent, virt_rows, turn, slab, local_cols):
    depth, lanes = sent.shape
    width = virt_rows.shape[1]
    chunks = slab // GROUP
    part = lanes // chunks
    return pl.pallas_call(
        last_kernel,
        grid=(chunks,),
        in_specs=[
            pl.BlockSpec(memory_space=pltpu.SMEM),
            pl.BlockSpec((depth, part), lambda c: (0, c)),
            pl.BlockSpec((depth, width), lambda c: (0, 0)),
        ],
        out_specs=pl.BlockSpec((GROUP, local_cols, width), lambda c: (c, 0, 0)),
        out_shape=jax.ShapeDtypeStruct((slab, local_cols, width), jnp.bfloat16),
        scratch_shapes=[pltpu.VMEM((part, width), jnp.float32)],
        compiler_params=pltpu.CompilerParams(vmem_limit_bytes=48 * 2**20),
        name="last_contract",
    )(turn, sent, virt_rows)


def panel_kernel(place_ref, occ_ref, virt_ref, table_ref, occ_out, virt_out):
    rows, width = occ_ref.shape
    count = table_ref.shape[1]
    size = width // count
    row = place_ref[0] * rows + lax.broadcasted_iota(jnp.int32, (rows, count), 0)
    first = lax.broadcasted_iota(jnp.int32, (rows, count), 1) * size
    pick = ((row >= first) & (row < first + size)).astype(jnp.float32)
    column = lax.broadcasted_iota(jnp.int32, (count, width), 1)
    first = lax.broadcasted_iota(jnp.int32, (count, width), 0) * size
    spread = ((column >= first) & (column < first + size)).astype(jnp.float32)

    def masked(ref, table):
        rows_kept = jnp.dot(pick, table.astype(jnp.float32), preferred_element_type=jnp.float32)
        kept = jnp.dot(rows_kept, spread, preferred_element_type=jnp.float32)
        return ref[...] * kept.astype(jnp.bfloat16)

    virt_out[...] = masked(virt_ref, table_ref[1])
    occ = masked(occ_ref, table_ref[0])
    for third in range(size // SUB):
        span = width // (size // SUB)
        source = lax.broadcasted_iota(jnp.int32, (width, span), 0)
        j = lax.broadcasted_iota(jnp.int32, (width, span), 1)
        wanted = (j // SUB) * size + third * SUB + j % SUB
        move = (source == wanted).astype(jnp.float32).astype(jnp.bfloat16)
        part = jnp.dot(occ, move, preferred_element_type=jnp.float32)
        occ_out[:, third * span : (third + 1) * span] = part.astype(jnp.bfloat16)


def panels(place, occ_green, virt_green, green_mask):
    whole = pl.BlockSpec(memory_space=pltpu.VMEM)
    return pl.pallas_call(
        panel_kernel,
        in_specs=[pl.BlockSpec(memory_space=pltpu.SMEM), whole, whole, whole],
        out_specs=[whole, whole],
        out_shape=[
            jax.ShapeDtypeStruct(occ_green.shape, jnp.bfloat16),
            jax.ShapeDtypeStruct(virt_green.shape, jnp.bfloat16),
        ],
        name="panels",
    )(place, occ_green, virt_green, green_mask)


def rows_kernel(core_ref, blocks_ref, own_ref, other_ref, out_ref, full_ref):
    core = core_ref[0]
    for panel in range(own_ref.shape[0] // PANEL):
        here = pl.ds(panel * PANEL, PANEL)
        for ref, place in ((own_ref, core), (other_ref, 1 - core)):
            first = pl.multiple_of((2 * panel + place) * PANEL, PANEL)
            full_ref[pl.ds(first, PANEL), :] = ref[here, :].astype(jnp.float32)
    count, size, _ = out_ref.shape
    for block in range(count):
        first = pl.multiple_of(blocks_ref[block] * size, SUB)
        out_ref[block] = full_ref[pl.ds(first, size), :].astype(jnp.bfloat16)


def block_rows(core, blocks, own, other, size):
    whole = pl.BlockSpec(memory_space=pltpu.VMEM)
    scalars = pl.BlockSpec(memory_space=pltpu.SMEM)
    depth, width = 2 * own.shape[0], own.shape[1]
    return pl.pallas_call(
        rows_kernel,
        in_specs=[scalars, scalars, whole, whole],
        out_specs=whole,
        out_shape=jax.ShapeDtypeStruct((depth // size, size, width), jnp.bfloat16),
        scratch_shapes=[pltpu.VMEM((depth, width), jnp.float32)],
        compiler_params=pltpu.CompilerParams(vmem_limit_bytes=32 * 2**20),
        name="block_rows",
    )(core, blocks, own, other)


def shards(three_centre, x_mask, occ_green, virt_green, green_mask, nu_blocks):
    nu_local, slab, width = three_centre.shape
    block_count = green_mask.shape[1]
    block_size = width // block_count
    groups = lax.axis_size("ri")
    members = lax.axis_size("ao")
    place = lax.axis_index("ao").astype(jnp.int32)
    core = (place % 2)[None]
    same_core = [[z * 2 + c for z in range(members // 2)] for c in range(2)]
    both_cores = [(a, a ^ 1) for a in range(members)]

    def gathered(panel):
        own = lax.all_gather(panel, "ao", axis=0, tiled=True, axis_index_groups=same_core)
        return own, lax.ppermute(own, "ao", both_cores)

    occ_panel, virt_panel = panels(place[None], occ_green, virt_green, green_mask)
    outgoing = half_contract(core, three_centre, x_mask, *gathered(occ_panel), groups)
    outgoing, virt_panel = lax.optimization_barrier((outgoing, virt_panel))
    sent = lax.all_to_all(outgoing, "ri", split_axis=0, concat_axis=0, tiled=True)
    virt_rows = block_rows(core, nu_blocks, *gathered(virt_panel), block_size).reshape(width, width)
    turn = (lax.axis_index("ri") % GROUP).astype(jnp.int32)[None]
    return last_contract(sent.reshape(width, -1), virt_rows, turn, slab, width // groups)


def solution(mesh):
    return jax.shard_map(
        shards,
        mesh=mesh,
        in_specs=(P("ri", "ao", None), P("ri", "ao", None), P("ao", None), P("ao", None), P(), P()),
        out_specs=P("ao", "ri", None),
        check_vma=False,
    )
```

```python
import functools

import jax
import jax.numpy as jnp
from jax import lax
from jax.experimental import pallas as pl
from jax.experimental.pallas import tpu as pltpu
from jax.sharding import PartitionSpec as P

LANES = 128
SUB = 8
GROUP = LANES // SUB
PANEL = 32


def exchange(parts):
    shape = parts[0].shape
    lane_group = lax.broadcasted_iota(jnp.int32, shape, 1) // SUB
    now = [pltpu.roll(part, SUB * p, 1) if p else part for p, part in enumerate(parts)]
    now = [now[(-k) % GROUP] for k in range(GROUP)]
    for bit in (1, 2, 4, 8):
        taken = (lane_group & bit) != 0
        now = [jnp.where(taken, now[(k - bit) % GROUP], now[k]) for k in range(GROUP)]
    return now


def widened(table, width):
    count = table.shape[1]
    size = width // count
    column = lax.broadcasted_iota(jnp.int32, (count, width), 1)
    first = lax.broadcasted_iota(jnp.int32, (count, width), 0) * size
    spread = ((column >= first) & (column < first + size)).astype(jnp.float32).astype(jnp.bfloat16)
    table = table.astype(jnp.float32).astype(jnp.bfloat16)
    return jnp.dot(table, spread, preferred_element_type=jnp.float32)


def half_kernel(core_ref, table_ref, own_ref, other_ref, x_hbm, out_ref, x_ref, keep_ref, occ_ref, half_ref, sems):
    chunk = pl.program_id(0)
    chunks, rows, slab, width = x_ref.shape
    groups = out_ref.shape[0]
    size = width // groups
    copies = [
        pltpu.make_async_copy(x_hbm.at[:, pl.ds(c * slab, slab), :], x_ref.at[c], sems.at[c])
        for c in range(chunks)
    ]

    def place(even_ref, odd_ref):
        for panel in range(width // PANEL):
            ref = odd_ref if panel % 2 else even_ref
            first = panel // 2 * PANEL
            blocks = [(panel * PANEL + row) // size for row in range(0, PANEL, SUB)]
            kept = jnp.concatenate([jnp.broadcast_to(keep_ref[i : i + 1, :], (SUB, width)) for i in blocks], 0)
            occ_ref[panel * PANEL : (panel + 1) * PANEL, :] = ref[first : first + PANEL, :] * kept.astype(jnp.bfloat16)

    @pl.when(chunk == 0)
    def _():
        for copy in copies:
            copy.start()
        keep_ref[...] = widened(table_ref[...], width)
        pl.when(core_ref[0] == 0)(lambda: place(own_ref, other_ref))
        pl.when(core_ref[0] != 0)(lambda: place(other_ref, own_ref))

    for c, copy in enumerate(copies):
        pl.when(chunk == c)(copy.wait)
    ri_rows = SUB
    ri_blocks = slab // ri_rows
    kept = jnp.concatenate(
        [
            jnp.broadcast_to(keep_ref[pl.ds(groups + chunk * ri_blocks + i, 1), :], (ri_rows, width))
            for i in range(ri_blocks)
        ],
        0,
    )
    masked = (x_ref[chunk] * kept.astype(jnp.bfloat16)[None]).reshape(rows * slab, width)
    span = 2 * LANES
    thirds = size // SUB
    for first in range(0, width, span):
        half = jnp.dot(masked, occ_ref[:, first : first + span], preferred_element_type=jnp.float32)
        for part in range(span // LANES):
            half_ref[first // LANES + part] = half[:, part * LANES : (part + 1) * LANES]
    for plane in range(width // LANES):
        part_ref = half_ref.at[plane]
        parts = [part_ref[pl.ds(p, rows, stride=slab), :] for p in range(slab)]
        for low, part in enumerate(exchange(parts)):
            group, third = divmod(plane * GROUP + low, thirds)
            out_ref[group, :, third * LANES : (third + 1) * LANES] = part.astype(jnp.bfloat16)


def last_kernel(turn_ref, sent_ref, virt_ref, out_ref, sum_ref):
    slab, local_cols, width = out_ref.shape
    part = sum_ref.shape[0]
    sent = sent_ref[:, pl.ds(pl.multiple_of(pl.program_id(0) * part, LANES), part)]
    sum_ref[...] = lax.dot_general(
        sent, virt_ref[...], (((0,), (0,)), ((), ())), preferred_element_type=jnp.float32
    )
    turn = turn_ref[0]
    for p in range(slab):
        pieces = [
            sum_ref[pl.ds(pl.multiple_of(third * LANES + lax.rem(p + turn + third, GROUP) * SUB, SUB), SUB), :]
            for third in range(local_cols // SUB)
        ]
        out_ref[p] = jnp.concatenate(pieces, 0).astype(jnp.bfloat16)


def half_contract(core, three_centre, table, own, other, groups):
    rows, slab, width = three_centre.shape
    chunks = slab // GROUP
    lanes = width // groups * GROUP
    whole = pl.BlockSpec(memory_space=pltpu.VMEM)
    return pl.pallas_call(
        half_kernel,
        grid=(chunks,),
        in_specs=[
            pl.BlockSpec(memory_space=pltpu.SMEM),
            whole,
            whole,
            whole,
            pl.BlockSpec(memory_space=pltpu.HBM),
        ],
        out_specs=pl.BlockSpec((groups, rows, lanes), lambda c: (0, 0, c)),
        out_shape=jax.ShapeDtypeStruct((groups, rows, chunks * lanes), jnp.bfloat16),
        scratch_shapes=[
            pltpu.VMEM((chunks, rows, GROUP, width), jnp.bfloat16),
            pltpu.VMEM((table.shape[0], width), jnp.float32),
            pltpu.VMEM((width, width), jnp.bfloat16),
            pltpu.VMEM((width // LANES, rows * GROUP, LANES), jnp.float32),
            pltpu.SemaphoreType.DMA((chunks,)),
        ],
        compiler_params=pltpu.CompilerParams(vmem_limit_bytes=51 * 2**20),
        name="half_contract",
    )(core, table, own, other, three_centre)


def last_contract(sent, virt_rows, turn, slab, local_cols):
    depth, lanes = sent.shape
    width = virt_rows.shape[1]
    chunks = slab // GROUP
    part = lanes // chunks
    return pl.pallas_call(
        last_kernel,
        grid=(chunks,),
        in_specs=[
            pl.BlockSpec(memory_space=pltpu.SMEM),
            pl.BlockSpec(memory_space=pltpu.VMEM),
            pl.BlockSpec(memory_space=pltpu.VMEM),
        ],
        out_specs=pl.BlockSpec((GROUP, local_cols, width), lambda c: (c, 0, 0)),
        out_shape=jax.ShapeDtypeStruct((slab, local_cols, width), jnp.bfloat16),
        scratch_shapes=[pltpu.VMEM((part, width), jnp.float32)],
        compiler_params=pltpu.CompilerParams(vmem_limit_bytes=48 * 2**20),
        name="last_contract",
    )(turn, sent, virt_rows)


def rows_kernel(core_ref, blocks_ref, table_ref, own_ref, other_ref, out_ref, full_ref, kept_ref):
    kept_ref[...] = widened(table_ref[1], own_ref.shape[1])
    core = core_ref[0]
    for panel in range(own_ref.shape[0] // PANEL):
        here = pl.ds(panel * PANEL, PANEL)
        for ref, place in ((own_ref, core), (other_ref, 1 - core)):
            first = pl.multiple_of((2 * panel + place) * PANEL, PANEL)
            full_ref[pl.ds(first, PANEL), :] = ref[here, :].astype(jnp.float32)
    count, size, _ = out_ref.shape
    for block in range(count):
        first = pl.multiple_of(blocks_ref[block] * size, SUB)
        kept = kept_ref[pl.ds(blocks_ref[block], 1), :]
        out_ref[block] = (full_ref[pl.ds(first, size), :] * kept).astype(jnp.bfloat16)


def block_rows(core, blocks, green_mask, own, other, size):
    whole = pl.BlockSpec(memory_space=pltpu.VMEM)
    scalars = pl.BlockSpec(memory_space=pltpu.SMEM)
    depth, width = 2 * own.shape[0], own.shape[1]
    return pl.pallas_call(
        rows_kernel,
        in_specs=[scalars, scalars, whole, whole, whole],
        out_specs=whole,
        out_shape=jax.ShapeDtypeStruct((depth // size, size, width), jnp.bfloat16),
        scratch_shapes=[
            pltpu.VMEM((depth, width), jnp.float32),
            pltpu.VMEM((green_mask.shape[1], width), jnp.float32),
        ],
        compiler_params=pltpu.CompilerParams(vmem_limit_bytes=32 * 2**20),
        name="block_rows",
    )(core, blocks, green_mask, own, other)


def shards(three_centre, x_mask, occ_green, virt_green, green_mask, nu_blocks):
    nu_local, slab, width = three_centre.shape
    block_count = green_mask.shape[1]
    block_size = width // block_count
    groups = lax.axis_size("ri")
    members = lax.axis_size("ao")
    place = lax.axis_index("ao").astype(jnp.int32)
    core = (place % 2)[None]
    same_core = [[z * 2 + c for z in range(members // 2)] for c in range(2)]
    both_cores = [(a, a ^ 1) for a in range(members)]

    def gather(panel):
        return lax.all_gather(panel, "ao", axis=0, tiled=True, axis_index_groups=same_core)

    def swap(half):
        return lax.ppermute(half, "ao", both_cores)

    own, kept, table = lax.optimization_barrier((gather(occ_green), x_mask, green_mask))
    blank = jnp.zeros((-kept.shape[1] % SUB, block_count), jnp.float32)
    table = jnp.concatenate([table[0].astype(jnp.float32), kept[0].astype(jnp.float32), blank], 0)
    outgoing = half_contract(core, three_centre, table, own, swap(own), groups)
    outgoing, virt_panel = lax.optimization_barrier((outgoing, virt_green))
    sent = lax.all_to_all(outgoing, "ri", split_axis=0, concat_axis=0, tiled=True)
    own = gather(virt_panel)
    virt_rows = block_rows(core, nu_blocks, green_mask, own, swap(own), block_size).reshape(width, width)
    turn = (lax.axis_index("ri") * (width // groups // SUB) % GROUP).astype(jnp.int32)[None]
    return last_contract(sent.reshape(width, -1), virt_rows, turn, slab, width // groups)


def solution(mesh):
    return jax.shard_map(
        shards,
        mesh=mesh,
        in_specs=(P("ri", "ao", None), P("ri", "ao", None), P("ao", None), P("ao", None), P(), P()),
        out_specs=P("ao", "ri", None),
        check_vma=False,
    )
```

```python
import functools

import jax
import jax.numpy as jnp
from jax import lax
from jax.experimental import pallas as pl
from jax.experimental.pallas import tpu as pltpu
from jax.sharding import PartitionSpec as P

LANES = 128
SUB = 8
GROUP = LANES // SUB
PANEL = 32


def exchange(parts):
    shape = parts[0].shape
    lane_group = lax.broadcasted_iota(jnp.int32, shape, 1) // SUB
    now = [pltpu.roll(part, SUB * p, 1) if p else part for p, part in enumerate(parts)]
    now = [now[(-k) % GROUP] for k in range(GROUP)]
    for bit in (1, 2, 4, 8):
        taken = (lane_group & bit) != 0
        now = [jnp.where(taken, now[(k - bit) % GROUP], now[k]) for k in range(GROUP)]
    return now


def widened(table, width):
    count = table.shape[1]
    size = width // count
    column = lax.broadcasted_iota(jnp.int32, (count, width), 1)
    first = lax.broadcasted_iota(jnp.int32, (count, width), 0) * size
    spread = ((column >= first) & (column < first + size)).astype(jnp.float32).astype(jnp.bfloat16)
    table = table.astype(jnp.float32).astype(jnp.bfloat16)
    return jnp.dot(table, spread, preferred_element_type=jnp.float32)


def half_kernel(core_ref, table_ref, own_ref, other_ref, x_hbm, out_hbm, x_ref, keep_ref, occ_ref, half_ref, out_ref, sems, out_sems):
    chunks, rows, slab, width = x_ref.shape
    groups = out_hbm.shape[0]
    size = width // groups
    copies = [
        pltpu.make_async_copy(x_hbm.at[:, pl.ds(c * slab, slab), :], x_ref.at[c], sems.at[c])
        for c in range(chunks)
    ]

    def place(even_ref, odd_ref):
        for panel in range(width // PANEL):
            ref = odd_ref if panel % 2 else even_ref
            first = panel // 2 * PANEL
            blocks = [(panel * PANEL + row) // size for row in range(0, PANEL, SUB)]
            kept = jnp.concatenate([jnp.broadcast_to(keep_ref[i : i + 1, :], (SUB, width)) for i in blocks], 0)
            occ_ref[panel * PANEL : (panel + 1) * PANEL, :] = ref[first : first + PANEL, :] * kept.astype(jnp.bfloat16)

    for copy in copies:
        copy.start()
    keep_ref[...] = widened(table_ref[...], width)
    pl.when(core_ref[0] == 0)(lambda: place(own_ref, other_ref))
    pl.when(core_ref[0] != 0)(lambda: place(other_ref, own_ref))

    span = 2 * LANES
    spans = width // span
    thirds = size // SUB
    lanes = thirds * LANES

    def masked(c):
        blocks = [groups + c * slab // SUB + i for i in range(slab // SUB)]
        kept = jnp.concatenate([jnp.broadcast_to(keep_ref[i : i + 1, :], (SUB, width)) for i in blocks], 0)
        return (x_ref[c] * kept.astype(jnp.bfloat16)[None]).reshape(rows * slab, width)

    def multiply(step, tensor):
        first = step % spans * span
        half = jnp.dot(tensor, occ_ref[:, first : first + span], preferred_element_type=jnp.float32)
        for part in range(span // LANES):
            half_ref[step % 2, part] = half[:, part * LANES : (part + 1) * LANES]

    def regroup(step):
        for part in range(span // LANES):
            plane = step % spans * (span // LANES) + part
            part_ref = half_ref.at[step % 2, part]
            parts = [part_ref[pl.ds(p, rows, stride=slab), :] for p in range(slab)]
            for low, piece in enumerate(exchange(parts)):
                group, third = divmod(plane * GROUP + low, thirds)
                first = step // spans * lanes + third * LANES
                out_ref[group, :, first : first + LANES] = piece.astype(jnp.bfloat16)

    out_copies = []
    for step in range(chunks * spans + 1):
        if step < chunks * spans:
            if step % spans == 0:
                copies[step // spans].wait()
                tensor = masked(step // spans)
            multiply(step, tensor)
        if step:
            regroup(step - 1)
        if step and step % spans == 0:
            these = pl.ds((step // spans - 1) * lanes, lanes)
            copy = pltpu.make_async_copy(
                out_ref.at[:, :, these], out_hbm.at[:, :, these], out_sems.at[step // spans - 1]
            )
            copy.start()
            out_copies.append(copy)
    for copy in out_copies:
        copy.wait()


def last_kernel(turn_ref, sent_ref, virt_ref, out_hbm, sum_ref, done_ref, sems):
    slab, local_cols, width = out_hbm.shape
    chunks = slab // GROUP
    part = sent_ref.shape[1] // chunks
    turn = turn_ref[0]

    def multiply(c):
        sum_ref[c] = lax.dot_general(
            sent_ref[:, c * part : (c + 1) * part],
            virt_ref[...],
            (((0,), (0,)), ((), ())),
            preferred_element_type=jnp.float32,
        )

    copies = []
    multiply(0)
    for c in range(chunks):
        if c + 1 < chunks:
            multiply(c + 1)
        for p in range(GROUP):
            pieces = [
                sum_ref[c, pl.ds(pl.multiple_of(third * LANES + lax.rem(p + turn + third, GROUP) * SUB, SUB), SUB), :]
                for third in range(local_cols // SUB)
            ]
            done_ref[c * GROUP + p] = jnp.concatenate(pieces, 0).astype(jnp.bfloat16)
        these = pl.ds(c * GROUP, GROUP)
        copies.append(pltpu.make_async_copy(done_ref.at[these], out_hbm.at[these], sems.at[c]))
        copies[-1].start()
    for copy in copies:
        copy.wait()


def half_contract(core, three_centre, table, own, other, groups):
    rows, slab, width = three_centre.shape
    chunks = slab // GROUP
    lanes = width // groups * GROUP
    whole = pl.BlockSpec(memory_space=pltpu.VMEM)
    return pl.pallas_call(
        half_kernel,
        in_specs=[
            pl.BlockSpec(memory_space=pltpu.SMEM),
            whole,
            whole,
            whole,
            pl.BlockSpec(memory_space=pltpu.HBM),
        ],
        out_specs=pl.BlockSpec(memory_space=pltpu.HBM),
        out_shape=jax.ShapeDtypeStruct((groups, rows, chunks * lanes), jnp.bfloat16),
        scratch_shapes=[
            pltpu.VMEM((chunks, rows, GROUP, width), jnp.bfloat16),
            pltpu.VMEM((table.shape[0], width), jnp.float32),
            pltpu.VMEM((width, width), jnp.bfloat16),
            pltpu.VMEM((2, 2, rows * GROUP, LANES), jnp.float32),
            pltpu.VMEM((groups, rows, chunks * lanes), jnp.bfloat16),
            pltpu.SemaphoreType.DMA((chunks,)),
            pltpu.SemaphoreType.DMA((chunks,)),
        ],
        compiler_params=pltpu.CompilerParams(vmem_limit_bytes=51 * 2**20),
        name="half_contract",
    )(core, table, own, other, three_centre)


def last_contract(sent, virt_rows, turn, slab, local_cols):
    lanes = sent.shape[1]
    width = virt_rows.shape[1]
    chunks = slab // GROUP
    whole = pl.BlockSpec(memory_space=pltpu.VMEM)
    return pl.pallas_call(
        last_kernel,
        in_specs=[pl.BlockSpec(memory_space=pltpu.SMEM), whole, whole],
        out_specs=pl.BlockSpec(memory_space=pltpu.HBM),
        out_shape=jax.ShapeDtypeStruct((slab, local_cols, width), jnp.bfloat16),
        scratch_shapes=[
            pltpu.VMEM((chunks, lanes // chunks, width), jnp.float32),
            pltpu.VMEM((slab, local_cols, width), jnp.bfloat16),
            pltpu.SemaphoreType.DMA((chunks,)),
        ],
        compiler_params=pltpu.CompilerParams(vmem_limit_bytes=48 * 2**20),
        name="last_contract",
    )(turn, sent, virt_rows)


def rows_kernel(core_ref, blocks_ref, table_ref, own_ref, other_ref, out_ref, full_ref, kept_ref):
    kept_ref[...] = widened(table_ref[1], own_ref.shape[1])
    core = core_ref[0]
    for panel in range(own_ref.shape[0] // PANEL):
        here = pl.ds(panel * PANEL, PANEL)
        for ref, place in ((own_ref, core), (other_ref, 1 - core)):
            first = pl.multiple_of((2 * panel + place) * PANEL, PANEL)
            full_ref[pl.ds(first, PANEL), :] = ref[here, :].astype(jnp.float32)
    count, size, _ = out_ref.shape
    for block in range(count):
        first = pl.multiple_of(blocks_ref[block] * size, SUB)
        kept = kept_ref[pl.ds(blocks_ref[block], 1), :]
        out_ref[block] = (full_ref[pl.ds(first, size), :] * kept).astype(jnp.bfloat16)


def block_rows(core, blocks, green_mask, own, other, size):
    whole = pl.BlockSpec(memory_space=pltpu.VMEM)
    scalars = pl.BlockSpec(memory_space=pltpu.SMEM)
    depth, width = 2 * own.shape[0], own.shape[1]
    return pl.pallas_call(
        rows_kernel,
        in_specs=[scalars, scalars, whole, whole, whole],
        out_specs=whole,
        out_shape=jax.ShapeDtypeStruct((depth // size, size, width), jnp.bfloat16),
        scratch_shapes=[
            pltpu.VMEM((depth, width), jnp.float32),
            pltpu.VMEM((green_mask.shape[1], width), jnp.float32),
        ],
        compiler_params=pltpu.CompilerParams(vmem_limit_bytes=32 * 2**20),
        name="block_rows",
    )(core, blocks, green_mask, own, other)


def shards(three_centre, x_mask, occ_green, virt_green, green_mask, nu_blocks):
    nu_local, slab, width = three_centre.shape
    block_count = green_mask.shape[1]
    block_size = width // block_count
    groups = lax.axis_size("ri")
    members = lax.axis_size("ao")
    place = lax.axis_index("ao").astype(jnp.int32)
    core = (place % 2)[None]
    same_core = [[z * 2 + c for z in range(members // 2)] for c in range(2)]
    both_cores = [(a, a ^ 1) for a in range(members)]

    def gather(panel):
        return lax.all_gather(panel, "ao", axis=0, tiled=True, axis_index_groups=same_core)

    def swap(half):
        return lax.ppermute(half, "ao", both_cores)

    own, kept, table = lax.optimization_barrier((gather(occ_green), x_mask, green_mask))
    blank = jnp.zeros((-kept.shape[1] % SUB, block_count), jnp.float32)
    table = jnp.concatenate([table[0].astype(jnp.float32), kept[0].astype(jnp.float32), blank], 0)
    outgoing = half_contract(core, three_centre, table, own, swap(own), groups)
    outgoing, virt_panel = lax.optimization_barrier((outgoing, virt_green))
    sent = lax.all_to_all(outgoing, "ri", split_axis=0, concat_axis=0, tiled=True)
    own = gather(virt_panel)
    virt_rows = block_rows(core, nu_blocks, green_mask, own, swap(own), block_size).reshape(width, width)
    turn = (lax.axis_index("ri") * (width // groups // SUB) % GROUP).astype(jnp.int32)[None]
    return last_contract(sent.reshape(width, -1), virt_rows, turn, slab, width // groups)


def solution(mesh):
    return jax.shard_map(
        shards,
        mesh=mesh,
        in_specs=(P("ri", "ao", None), P("ri", "ao", None), P("ao", None), P("ao", None), P(), P()),
        out_specs=P("ao", "ri", None),
        check_vma=False,
    )
```

```python
import functools

import jax
import jax.numpy as jnp
from jax import lax
from jax.experimental import pallas as pl
from jax.experimental.pallas import tpu as pltpu
from jax.sharding import PartitionSpec as P

LANES = 128
SUB = 8
GROUP = LANES // SUB
PANEL = 32
LEAVE = 8


def exchange(parts):
    shape = parts[0].shape
    lane_group = lax.broadcasted_iota(jnp.int32, shape, 1) // SUB
    now = [pltpu.roll(part, SUB * p, 1) if p else part for p, part in enumerate(parts)]
    now = [now[(-k) % GROUP] for k in range(GROUP)]
    for bit in (1, 2, 4, 8):
        taken = (lane_group & bit) != 0
        now = [jnp.where(taken, now[(k - bit) % GROUP], now[k]) for k in range(GROUP)]
    return now


def widened(table, width):
    count = table.shape[1]
    size = width // count
    column = lax.broadcasted_iota(jnp.int32, (count, width), 1)
    first = lax.broadcasted_iota(jnp.int32, (count, width), 0) * size
    spread = ((column >= first) & (column < first + size)).astype(jnp.float32).astype(jnp.bfloat16)
    table = table.astype(jnp.float32).astype(jnp.bfloat16)
    return jnp.dot(table, spread, preferred_element_type=jnp.float32)


def half_kernel(core_ref, table_ref, own_ref, other_ref, x_hbm, out_hbm, x_ref, keep_ref, occ_ref, half_ref, out_ref, sems, out_sems):
    chunks, rows, slab, width = x_ref.shape
    groups = out_hbm.shape[0]
    size = width // groups
    copies = [
        pltpu.make_async_copy(x_hbm.at[:, pl.ds(c * slab, slab), :], x_ref.at[c], sems.at[c])
        for c in range(chunks)
    ]

    def place(even_ref, odd_ref):
        for panel in range(width // PANEL):
            ref = odd_ref if panel % 2 else even_ref
            first = panel // 2 * PANEL
            blocks = [(panel * PANEL + row) // size for row in range(0, PANEL, SUB)]
            kept = jnp.concatenate([jnp.broadcast_to(keep_ref[i : i + 1, :], (SUB, width)) for i in blocks], 0)
            occ_ref[panel * PANEL : (panel + 1) * PANEL, :] = ref[first : first + PANEL, :] * kept.astype(jnp.bfloat16)

    copies[0].start()
    keep_ref[...] = widened(table_ref[...], width)
    pl.when(core_ref[0] == 0)(lambda: place(own_ref, other_ref))
    pl.when(core_ref[0] != 0)(lambda: place(other_ref, own_ref))

    span = 2 * LANES
    spans = width // span
    thirds = size // SUB
    lanes = thirds * LANES

    def masked(c):
        blocks = [groups + c * slab // SUB + i for i in range(slab // SUB)]
        kept = jnp.concatenate([jnp.broadcast_to(keep_ref[i : i + 1, :], (SUB, width)) for i in blocks], 0)
        return (x_ref[c] * kept.astype(jnp.bfloat16)[None]).reshape(rows * slab, width)

    def multiply(step, tensor):
        first = step % spans * span
        half = jnp.dot(tensor, occ_ref[:, first : first + span], preferred_element_type=jnp.float32)
        for part in range(span // LANES):
            half_ref[step % 2, part] = half[:, part * LANES : (part + 1) * LANES]

    def regroup(step):
        for part in range(span // LANES):
            plane = step % spans * (span // LANES) + part
            part_ref = half_ref.at[step % 2, part]
            parts = [part_ref[pl.ds(p, rows, stride=slab), :] for p in range(slab)]
            for low, piece in enumerate(exchange(parts)):
                group, third = divmod(plane * GROUP + low, thirds)
                first = step // spans * lanes + third * LANES
                out_ref[group, :, first : first + LANES] = piece.astype(jnp.bfloat16)

    out_copies = []
    for step in range(chunks * spans + 1):
        if step < chunks * spans:
            if step % spans == 0:
                copies[step // spans].wait()
                if step == 0:
                    for copy in copies[1:]:
                        copy.start()
                tensor = masked(step // spans)
            multiply(step, tensor)
        if step:
            regroup(step - 1)
        if step:
            chunk, part = divmod(step - 1, spans)
            ready = [i * span // SUB // thirds for i in (part, part + 1)]
            these = pl.ds(ready[0], ready[1] - ready[0]), slice(None), pl.ds(chunk * lanes, lanes)
            copy = pltpu.make_async_copy(out_ref.at[these], out_hbm.at[these], out_sems.at[step - 1])
            copy.start()
            out_copies.append(copy)
    for copy in out_copies:
        copy.wait()


def last_kernel(turn_ref, sent_ref, virt_ref, out_hbm, sum_ref, done_ref, sems):
    slab, local_cols, width = out_hbm.shape
    chunks = slab // GROUP
    part = sent_ref.shape[1] // chunks
    turn = turn_ref[0]

    def multiply(c):
        sum_ref[c] = lax.dot_general(
            sent_ref[:, c * part : (c + 1) * part],
            virt_ref[...],
            (((0,), (0,)), ((), ())),
            preferred_element_type=jnp.float32,
        )

    copies = []
    multiply(0)
    for c in range(chunks):
        if c + 1 < chunks:
            multiply(c + 1)
        for p in range(GROUP):
            pieces = [
                sum_ref[c, pl.ds(pl.multiple_of(third * LANES + lax.rem(p + turn + third, GROUP) * SUB, SUB), SUB), :]
                for third in range(local_cols // SUB)
            ]
            done_ref[c * GROUP + p] = jnp.concatenate(pieces, 0).astype(jnp.bfloat16)
            if (p + 1) % LEAVE == 0:
                these = pl.ds(c * GROUP + p + 1 - LEAVE, LEAVE)
                copies.append(pltpu.make_async_copy(done_ref.at[these], out_hbm.at[these], sems.at[len(copies)]))
                copies[-1].start()
    for copy in copies:
        copy.wait()


def half_contract(core, three_centre, table, own, other, groups):
    rows, slab, width = three_centre.shape
    chunks = slab // GROUP
    lanes = width // groups * GROUP
    whole = pl.BlockSpec(memory_space=pltpu.VMEM)
    return pl.pallas_call(
        half_kernel,
        in_specs=[
            pl.BlockSpec(memory_space=pltpu.SMEM),
            whole,
            whole,
            whole,
            pl.BlockSpec(memory_space=pltpu.HBM),
        ],
        out_specs=pl.BlockSpec(memory_space=pltpu.HBM),
        out_shape=jax.ShapeDtypeStruct((groups, rows, chunks * lanes), jnp.bfloat16),
        scratch_shapes=[
            pltpu.VMEM((chunks, rows, GROUP, width), jnp.bfloat16),
            pltpu.VMEM((table.shape[0], width), jnp.float32),
            pltpu.VMEM((width, width), jnp.bfloat16),
            pltpu.VMEM((2, 2, rows * GROUP, LANES), jnp.float32),
            pltpu.VMEM((groups, rows, chunks * lanes), jnp.bfloat16),
            pltpu.SemaphoreType.DMA((chunks,)),
            pltpu.SemaphoreType.DMA((chunks * width // (2 * LANES),)),
        ],
        compiler_params=pltpu.CompilerParams(vmem_limit_bytes=51 * 2**20),
        name="half_contract",
    )(core, table, own, other, three_centre)


def last_contract(sent, virt_rows, turn, slab, local_cols):
    lanes = sent.shape[1]
    width = virt_rows.shape[1]
    chunks = slab // GROUP
    whole = pl.BlockSpec(memory_space=pltpu.VMEM)
    return pl.pallas_call(
        last_kernel,
        in_specs=[pl.BlockSpec(memory_space=pltpu.SMEM), whole, whole],
        out_specs=pl.BlockSpec(memory_space=pltpu.HBM),
        out_shape=jax.ShapeDtypeStruct((slab, local_cols, width), jnp.bfloat16),
        scratch_shapes=[
            pltpu.VMEM((chunks, lanes // chunks, width), jnp.float32),
            pltpu.VMEM((slab, local_cols, width), jnp.bfloat16),
            pltpu.SemaphoreType.DMA((slab // LEAVE,)),
        ],
        compiler_params=pltpu.CompilerParams(vmem_limit_bytes=48 * 2**20),
        name="last_contract",
    )(turn, sent, virt_rows)


def rows_kernel(core_ref, blocks_ref, table_ref, own_ref, other_ref, out_ref, full_ref, kept_ref):
    kept_ref[...] = widened(table_ref[1], own_ref.shape[1])
    core = core_ref[0]
    for panel in range(own_ref.shape[0] // PANEL):
        here = pl.ds(panel * PANEL, PANEL)
        for ref, place in ((own_ref, core), (other_ref, 1 - core)):
            first = pl.multiple_of((2 * panel + place) * PANEL, PANEL)
            full_ref[pl.ds(first, PANEL), :] = ref[here, :].astype(jnp.float32)
    count, size, _ = out_ref.shape
    for block in range(count):
        first = pl.multiple_of(blocks_ref[block] * size, SUB)
        kept = kept_ref[pl.ds(blocks_ref[block], 1), :]
        out_ref[block] = (full_ref[pl.ds(first, size), :] * kept).astype(jnp.bfloat16)


def block_rows(core, blocks, green_mask, own, other, size):
    whole = pl.BlockSpec(memory_space=pltpu.VMEM)
    scalars = pl.BlockSpec(memory_space=pltpu.SMEM)
    depth, width = 2 * own.shape[0], own.shape[1]
    return pl.pallas_call(
        rows_kernel,
        in_specs=[scalars, scalars, whole, whole, whole],
        out_specs=whole,
        out_shape=jax.ShapeDtypeStruct((depth // size, size, width), jnp.bfloat16),
        scratch_shapes=[
            pltpu.VMEM((depth, width), jnp.float32),
            pltpu.VMEM((green_mask.shape[1], width), jnp.float32),
        ],
        compiler_params=pltpu.CompilerParams(vmem_limit_bytes=32 * 2**20),
        name="block_rows",
    )(core, blocks, green_mask, own, other)


def shards(three_centre, x_mask, occ_green, virt_green, green_mask, nu_blocks):
    nu_local, slab, width = three_centre.shape
    block_count = green_mask.shape[1]
    block_size = width // block_count
    groups = lax.axis_size("ri")
    members = lax.axis_size("ao")
    place = lax.axis_index("ao").astype(jnp.int32)
    core = (place % 2)[None]
    same_core = [[z * 2 + c for z in range(members // 2)] for c in range(2)]
    both_cores = [(a, a ^ 1) for a in range(members)]

    def gather(panel):
        return lax.all_gather(panel, "ao", axis=0, tiled=True, axis_index_groups=same_core)

    def swap(half):
        return lax.ppermute(half, "ao", both_cores)

    own, kept, table = lax.optimization_barrier((gather(occ_green), x_mask, green_mask))
    blank = jnp.zeros((-kept.shape[1] % SUB, block_count), jnp.float32)
    table = jnp.concatenate([table[0].astype(jnp.float32), kept[0].astype(jnp.float32), blank], 0)
    outgoing = half_contract(core, three_centre, table, own, swap(own), groups)
    outgoing, virt_panel = lax.optimization_barrier((outgoing, virt_green))
    sent = lax.all_to_all(outgoing, "ri", split_axis=0, concat_axis=0, tiled=True)
    own = gather(virt_panel)
    virt_rows = block_rows(core, nu_blocks, green_mask, own, swap(own), block_size).reshape(width, width)
    turn = (lax.axis_index("ri") * (width // groups // SUB) % GROUP).astype(jnp.int32)[None]
    return last_contract(sent.reshape(width, -1), virt_rows, turn, slab, width // groups)


def solution(mesh):
    return jax.shard_map(
        shards,
        mesh=mesh,
        in_specs=(P("ri", "ao", None), P("ri", "ao", None), P("ao", None), P("ao", None), P(), P()),
        out_specs=P("ao", "ri", None),
        check_vma=False,
    )
```

```python
import functools

import jax
import jax.numpy as jnp
from jax import lax
from jax.experimental import pallas as pl
from jax.experimental.pallas import tpu as pltpu
from jax.sharding import PartitionSpec as P

LANES = 128
SUB = 8
GROUP = LANES // SUB
PANEL = 32
PIECE = 6


def exchange(parts):
    shape = parts[0].shape
    lane_group = lax.broadcasted_iota(jnp.int32, shape, 1) // SUB
    now = [pltpu.roll(part, SUB * p, 1) if p else part for p, part in enumerate(parts)]
    now = [now[(-k) % GROUP] for k in range(GROUP)]
    for bit in (1, 2, 4, 8):
        taken = (lane_group & bit) != 0
        now = [jnp.where(taken, now[(k - bit) % GROUP], now[k]) for k in range(GROUP)]
    return now


def widened(table, width):
    count = table.shape[1]
    size = width // count
    column = lax.broadcasted_iota(jnp.int32, (count, width), 1)
    first = lax.broadcasted_iota(jnp.int32, (count, width), 0) * size
    spread = ((column >= first) & (column < first + size)).astype(jnp.float32).astype(jnp.bfloat16)
    table = table.astype(jnp.float32).astype(jnp.bfloat16)
    return jnp.dot(table, spread, preferred_element_type=jnp.float32)


def mask_kernel(core_ref, kept_ref, x_hbm, out_ref, sems):
    del core_ref
    rows, slab, width = out_ref.shape
    chunks, in_chunk, count = kept_ref.shape
    ri_blocks = chunks * in_chunk
    pieces = [pl.ds(first, PIECE) for first in range(0, rows, PIECE)]
    copies = [pltpu.make_async_copy(x_hbm.at[r], out_ref.at[r], sems.at[i]) for i, r in enumerate(pieces)]
    for copy in copies:
        copy.start()
    block = lax.broadcasted_iota(jnp.int32, (slab // ri_blocks, width), 1) // (width // count)
    kept = []
    for i in range(ri_blocks):
        word = jnp.int32(0)
        for b in range(count):
            word = word | (kept_ref[i // in_chunk, i % in_chunk, b] << b)
        kept.append(lax.shift_right_logical(jnp.full(block.shape, word), block) & 1)
    kept = jnp.concatenate(kept, 0).astype(jnp.float32).astype(jnp.bfloat16)
    for r, copy in zip(pieces, copies):
        copy.wait()
        out_ref[r] = out_ref[r] * kept[None]


def half_kernel(core_ref, table_ref, own_ref, other_ref, x_ref, out_hbm, keep_ref, occ_ref, half_ref, out_ref, out_sems):
    rows, ri_rows, width = x_ref.shape
    slab = GROUP
    chunks = ri_rows // slab
    groups = out_hbm.shape[0]
    size = width // groups

    def place(even_ref, odd_ref):
        for panel in range(width // PANEL):
            ref = odd_ref if panel % 2 else even_ref
            first = panel // 2 * PANEL
            blocks = [(panel * PANEL + row) // size for row in range(0, PANEL, SUB)]
            kept = jnp.concatenate([jnp.broadcast_to(keep_ref[i : i + 1, :], (SUB, width)) for i in blocks], 0)
            occ_ref[panel * PANEL : (panel + 1) * PANEL, :] = ref[first : first + PANEL, :] * kept.astype(jnp.bfloat16)

    keep_ref[...] = widened(table_ref[...], width)
    pl.when(core_ref[0] == 0)(lambda: place(own_ref, other_ref))
    pl.when(core_ref[0] != 0)(lambda: place(other_ref, own_ref))

    span = 2 * LANES
    spans = width // span
    thirds = size // SUB
    lanes = thirds * LANES

    def multiply(step, tensor):
        first = step % spans * span
        half = jnp.dot(tensor, occ_ref[:, first : first + span], preferred_element_type=jnp.float32)
        for part in range(span // LANES):
            half_ref[step % 2, part] = half[:, part * LANES : (part + 1) * LANES]

    def regroup(step):
        for part in range(span // LANES):
            plane = step % spans * (span // LANES) + part
            part_ref = half_ref.at[step % 2, part]
            parts = [part_ref[pl.ds(p, rows, stride=slab), :] for p in range(slab)]
            for low, piece in enumerate(exchange(parts)):
                group, third = divmod(plane * GROUP + low, thirds)
                first = step // spans * lanes + third * LANES
                out_ref[group, :, first : first + LANES] = piece.astype(jnp.bfloat16)

    out_copies = []
    for step in range(chunks * spans + 1):
        if step < chunks * spans:
            if step % spans == 0:
                first = step // spans * slab
                tensor = x_ref[:, first : first + slab, :].reshape(rows * slab, width)
            multiply(step, tensor)
        if step:
            regroup(step - 1)
        if step and step % spans == 0:
            these = pl.ds((step // spans - 1) * lanes, lanes)
            copy = pltpu.make_async_copy(
                out_ref.at[:, :, these], out_hbm.at[:, :, these], out_sems.at[step // spans - 1]
            )
            copy.start()
            out_copies.append(copy)
    for copy in out_copies:
        copy.wait()


def last_kernel(turn_ref, sent_ref, virt_ref, out_hbm, sum_ref, done_ref, sems):
    slab, local_cols, width = out_hbm.shape
    chunks = slab // GROUP
    part = sent_ref.shape[1] // chunks
    turn = turn_ref[0]

    def multiply(c):
        sum_ref[c] = lax.dot_general(
            sent_ref[:, c * part : (c + 1) * part],
            virt_ref[...],
            (((0,), (0,)), ((), ())),
            preferred_element_type=jnp.float32,
        )

    copies = []
    multiply(0)
    for c in range(chunks):
        if c + 1 < chunks:
            multiply(c + 1)
        for p in range(GROUP):
            pieces = [
                sum_ref[c, pl.ds(pl.multiple_of(third * LANES + lax.rem(p + turn + third, GROUP) * SUB, SUB), SUB), :]
                for third in range(local_cols // SUB)
            ]
            done_ref[c * GROUP + p] = jnp.concatenate(pieces, 0).astype(jnp.bfloat16)
        these = pl.ds(c * GROUP, GROUP)
        copies.append(pltpu.make_async_copy(done_ref.at[these], out_hbm.at[these], sems.at[c]))
        copies[-1].start()
    for copy in copies:
        copy.wait()


def mask_tensor(core, three_centre, x_mask):
    rows, slab, _ = three_centre.shape
    scalars = pl.BlockSpec(memory_space=pltpu.SMEM)
    return pl.pallas_call(
        mask_kernel,
        in_specs=[scalars, scalars, pl.BlockSpec(memory_space=pltpu.HBM)],
        out_specs=pl.BlockSpec(memory_space=pltpu.VMEM),
        out_shape=jax.ShapeDtypeStruct(three_centre.shape, jnp.bfloat16),
        scratch_shapes=[pltpu.SemaphoreType.DMA((rows // PIECE,))],
        compiler_params=pltpu.CompilerParams(vmem_limit_bytes=51 * 2**20),
        name="mask_tensor",
    )(core, x_mask.reshape(slab // GROUP, -1, x_mask.shape[-1]), three_centre)


def half_contract(core, masked, table, own, other, groups):
    rows, slab, width = masked.shape
    chunks = slab // GROUP
    lanes = width // groups * GROUP
    whole = pl.BlockSpec(memory_space=pltpu.VMEM)
    return pl.pallas_call(
        half_kernel,
        in_specs=[
            pl.BlockSpec(memory_space=pltpu.SMEM),
            whole,
            whole,
            whole,
            whole,
        ],
        out_specs=pl.BlockSpec(memory_space=pltpu.HBM),
        out_shape=jax.ShapeDtypeStruct((groups, rows, chunks * lanes), jnp.bfloat16),
        scratch_shapes=[
            pltpu.VMEM((table.shape[0], width), jnp.float32),
            pltpu.VMEM((width, width), jnp.bfloat16),
            pltpu.VMEM((2, 2, rows * GROUP, LANES), jnp.float32),
            pltpu.VMEM((groups, rows, chunks * lanes), jnp.bfloat16),
            pltpu.SemaphoreType.DMA((chunks,)),
        ],
        compiler_params=pltpu.CompilerParams(vmem_limit_bytes=32 * 2**20),
        name="half_contract",
    )(core, table, own, other, masked)


def last_contract(sent, virt_rows, turn, slab, local_cols):
    lanes = sent.shape[1]
    width = virt_rows.shape[1]
    chunks = slab // GROUP
    whole = pl.BlockSpec(memory_space=pltpu.VMEM)
    return pl.pallas_call(
        last_kernel,
        in_specs=[pl.BlockSpec(memory_space=pltpu.SMEM), whole, whole],
        out_specs=pl.BlockSpec(memory_space=pltpu.HBM),
        out_shape=jax.ShapeDtypeStruct((slab, local_cols, width), jnp.bfloat16),
        scratch_shapes=[
            pltpu.VMEM((chunks, lanes // chunks, width), jnp.float32),
            pltpu.VMEM((slab, local_cols, width), jnp.bfloat16),
            pltpu.SemaphoreType.DMA((chunks,)),
        ],
        compiler_params=pltpu.CompilerParams(vmem_limit_bytes=48 * 2**20),
        name="last_contract",
    )(turn, sent, virt_rows)


def rows_kernel(core_ref, blocks_ref, table_ref, own_ref, other_ref, out_ref, full_ref, kept_ref):
    kept_ref[...] = widened(table_ref[1], own_ref.shape[1])
    core = core_ref[0]
    for panel in range(own_ref.shape[0] // PANEL):
        here = pl.ds(panel * PANEL, PANEL)
        for ref, place in ((own_ref, core), (other_ref, 1 - core)):
            first = pl.multiple_of((2 * panel + place) * PANEL, PANEL)
            full_ref[pl.ds(first, PANEL), :] = ref[here, :].astype(jnp.float32)
    count, size, _ = out_ref.shape
    for block in range(count):
        first = pl.multiple_of(blocks_ref[block] * size, SUB)
        kept = kept_ref[pl.ds(blocks_ref[block], 1), :]
        out_ref[block] = (full_ref[pl.ds(first, size), :] * kept).astype(jnp.bfloat16)


def block_rows(core, blocks, green_mask, own, other, size):
    whole = pl.BlockSpec(memory_space=pltpu.VMEM)
    scalars = pl.BlockSpec(memory_space=pltpu.SMEM)
    depth, width = 2 * own.shape[0], own.shape[1]
    return pl.pallas_call(
        rows_kernel,
        in_specs=[scalars, scalars, whole, whole, whole],
        out_specs=whole,
        out_shape=jax.ShapeDtypeStruct((depth // size, size, width), jnp.bfloat16),
        scratch_shapes=[
            pltpu.VMEM((depth, width), jnp.float32),
            pltpu.VMEM((green_mask.shape[1], width), jnp.float32),
        ],
        compiler_params=pltpu.CompilerParams(vmem_limit_bytes=32 * 2**20),
        name="block_rows",
    )(core, blocks, green_mask, own, other)


def shards(three_centre, x_mask, occ_green, virt_green, green_mask, nu_blocks):
    nu_local, slab, width = three_centre.shape
    block_count = green_mask.shape[1]
    block_size = width // block_count
    groups = lax.axis_size("ri")
    members = lax.axis_size("ao")
    place = lax.axis_index("ao").astype(jnp.int32)
    core = (place % 2)[None]
    same_core = [[z * 2 + c for z in range(members // 2)] for c in range(2)]
    both_cores = [(a, a ^ 1) for a in range(members)]

    def gather(panel):
        return lax.all_gather(panel, "ao", axis=0, tiled=True, axis_index_groups=same_core)

    def swap(half):
        return lax.ppermute(half, "ao", both_cores)

    own, after, table = lax.optimization_barrier((gather(occ_green), core, green_mask))
    masked = mask_tensor(after, three_centre, x_mask)
    table = table[0].astype(jnp.float32)
    outgoing = half_contract(core, masked, table, own, swap(own), groups)
    outgoing, virt_panel = lax.optimization_barrier((outgoing, virt_green))
    sent = lax.all_to_all(outgoing, "ri", split_axis=0, concat_axis=0, tiled=True)
    own = gather(virt_panel)
    virt_rows = block_rows(core, nu_blocks, green_mask, own, swap(own), block_size).reshape(width, width)
    turn = (lax.axis_index("ri") * (width // groups // SUB) % GROUP).astype(jnp.int32)[None]
    return last_contract(sent.reshape(width, -1), virt_rows, turn, slab, width // groups)


def solution(mesh):
    return jax.shard_map(
        shards,
        mesh=mesh,
        in_specs=(P("ri", "ao", None), P("ri", "ao", None), P("ao", None), P("ao", None), P(), P()),
        out_specs=P("ao", "ri", None),
        check_vma=False,
    )
```

```python
import functools

import jax
import jax.numpy as jnp
from jax import lax
from jax.experimental import pallas as pl
from jax.experimental.pallas import tpu as pltpu
from jax.sharding import PartitionSpec as P

LANES = 128
SUB = 8
GROUP = LANES // SUB
PANEL = 32
PIECE = 6


def exchange(parts):
    shape = parts[0].shape
    lane_group = lax.broadcasted_iota(jnp.int32, shape, 1) // SUB
    now = [pltpu.roll(part, SUB * p, 1) if p else part for p, part in enumerate(parts)]
    now = [now[(-k) % GROUP] for k in range(GROUP)]
    for bit in (1, 2, 4, 8):
        taken = (lane_group & bit) != 0
        now = [jnp.where(taken, now[(k - bit) % GROUP], now[k]) for k in range(GROUP)]
    return now


def widened(table, width):
    count = table.shape[1]
    size = width // count
    column = lax.broadcasted_iota(jnp.int32, (count, width), 1)
    first = lax.broadcasted_iota(jnp.int32, (count, width), 0) * size
    spread = ((column >= first) & (column < first + size)).astype(jnp.float32).astype(jnp.bfloat16)
    table = table.astype(jnp.float32).astype(jnp.bfloat16)
    return jnp.dot(table, spread, preferred_element_type=jnp.float32)


def fetch_kernel(core_ref, x_hbm, out_ref, sems):
    del core_ref
    pieces = [pl.ds(first, PIECE) for first in range(0, out_ref.shape[0], PIECE)]
    copies = [pltpu.make_async_copy(x_hbm.at[r], out_ref.at[r], sems.at[i]) for i, r in enumerate(pieces)]
    for copy in copies:
        copy.start()
    for copy in copies:
        copy.wait()


def half_kernel(core_ref, table_ref, own_ref, other_ref, x_ref, out_hbm, keep_ref, occ_ref, half_ref, out_ref, out_sems):
    rows, ri_rows, width = x_ref.shape
    slab = GROUP
    chunks = ri_rows // slab
    groups = out_hbm.shape[0]
    size = width // groups

    def place(even_ref, odd_ref):
        for panel in range(width // PANEL):
            ref = odd_ref if panel % 2 else even_ref
            first = panel // 2 * PANEL
            blocks = [(panel * PANEL + row) // size for row in range(0, PANEL, SUB)]
            kept = jnp.concatenate([jnp.broadcast_to(keep_ref[i : i + 1, :], (SUB, width)) for i in blocks], 0)
            occ_ref[panel * PANEL : (panel + 1) * PANEL, :] = ref[first : first + PANEL, :] * kept.astype(jnp.bfloat16)

    keep_ref[...] = widened(table_ref[...], width)
    pl.when(core_ref[0] == 0)(lambda: place(own_ref, other_ref))
    pl.when(core_ref[0] != 0)(lambda: place(other_ref, own_ref))

    span = 2 * LANES
    spans = width // span
    thirds = size // SUB
    lanes = thirds * LANES

    def masked(c):
        blocks = [groups + c * slab // SUB + i for i in range(slab // SUB)]
        kept = jnp.concatenate([jnp.broadcast_to(keep_ref[i : i + 1, :], (SUB, width)) for i in blocks], 0)
        return (x_ref[:, c * slab : (c + 1) * slab, :] * kept.astype(jnp.bfloat16)[None]).reshape(rows * slab, width)

    def multiply(step, tensor):
        first = step % spans * span
        half = jnp.dot(tensor, occ_ref[:, first : first + span], preferred_element_type=jnp.float32)
        for part in range(span // LANES):
            half_ref[step % 2, part] = half[:, part * LANES : (part + 1) * LANES]

    def regroup(step):
        for part in range(span // LANES):
            plane = step % spans * (span // LANES) + part
            part_ref = half_ref.at[step % 2, part]
            parts = [part_ref[pl.ds(p, rows, stride=slab), :] for p in range(slab)]
            for low, piece in enumerate(exchange(parts)):
                group, third = divmod(plane * GROUP + low, thirds)
                first = step // spans * lanes + third * LANES
                out_ref[group, :, first : first + LANES] = piece.astype(jnp.bfloat16)

    out_copies = []
    for step in range(chunks * spans + 1):
        if step < chunks * spans:
            if step % spans == 0:
                tensor = masked(step // spans)
            multiply(step, tensor)
        if step:
            regroup(step - 1)
        if step and step % spans == 0:
            these = pl.ds((step // spans - 1) * lanes, lanes)
            copy = pltpu.make_async_copy(
                out_ref.at[:, :, these], out_hbm.at[:, :, these], out_sems.at[step // spans - 1]
            )
            copy.start()
            out_copies.append(copy)
    for copy in out_copies:
        copy.wait()


def last_kernel(turn_ref, sent_ref, virt_ref, out_hbm, sum_ref, done_ref, sems):
    slab, local_cols, width = out_hbm.shape
    chunks = slab // GROUP
    part = sent_ref.shape[1] // chunks
    turn = turn_ref[0]

    def multiply(c):
        sum_ref[c] = lax.dot_general(
            sent_ref[:, c * part : (c + 1) * part],
            virt_ref[...],
            (((0,), (0,)), ((), ())),
            preferred_element_type=jnp.float32,
        )

    copies = []
    multiply(0)
    for c in range(chunks):
        if c + 1 < chunks:
            multiply(c + 1)
        for p in range(GROUP):
            pieces = [
                sum_ref[c, pl.ds(pl.multiple_of(third * LANES + lax.rem(p + turn + third, GROUP) * SUB, SUB), SUB), :]
                for third in range(local_cols // SUB)
            ]
            done_ref[c * GROUP + p] = jnp.concatenate(pieces, 0).astype(jnp.bfloat16)
        these = pl.ds(c * GROUP, GROUP)
        copies.append(pltpu.make_async_copy(done_ref.at[these], out_hbm.at[these], sems.at[c]))
        copies[-1].start()
    for copy in copies:
        copy.wait()


def fetch(core, three_centre):
    return pl.pallas_call(
        fetch_kernel,
        in_specs=[pl.BlockSpec(memory_space=pltpu.SMEM), pl.BlockSpec(memory_space=pltpu.HBM)],
        out_specs=pl.BlockSpec(memory_space=pltpu.VMEM),
        out_shape=jax.ShapeDtypeStruct(three_centre.shape, jnp.bfloat16),
        scratch_shapes=[pltpu.SemaphoreType.DMA((three_centre.shape[0] // PIECE,))],
        compiler_params=pltpu.CompilerParams(vmem_limit_bytes=51 * 2**20),
        name="fetch",
    )(core, three_centre)


def half_contract(core, three_centre, table, own, other, groups):
    rows, slab, width = three_centre.shape
    chunks = slab // GROUP
    lanes = width // groups * GROUP
    whole = pl.BlockSpec(memory_space=pltpu.VMEM)
    return pl.pallas_call(
        half_kernel,
        in_specs=[
            pl.BlockSpec(memory_space=pltpu.SMEM),
            whole,
            whole,
            whole,
            whole,
        ],
        out_specs=pl.BlockSpec(memory_space=pltpu.HBM),
        out_shape=jax.ShapeDtypeStruct((groups, rows, chunks * lanes), jnp.bfloat16),
        scratch_shapes=[
            pltpu.VMEM((table.shape[0], width), jnp.float32),
            pltpu.VMEM((width, width), jnp.bfloat16),
            pltpu.VMEM((2, 2, rows * GROUP, LANES), jnp.float32),
            pltpu.VMEM((groups, rows, chunks * lanes), jnp.bfloat16),
            pltpu.SemaphoreType.DMA((chunks,)),
        ],
        compiler_params=pltpu.CompilerParams(vmem_limit_bytes=32 * 2**20),
        name="half_contract",
    )(core, table, own, other, three_centre)


def last_contract(sent, virt_rows, turn, slab, local_cols):
    lanes = sent.shape[1]
    width = virt_rows.shape[1]
    chunks = slab // GROUP
    whole = pl.BlockSpec(memory_space=pltpu.VMEM)
    return pl.pallas_call(
        last_kernel,
        in_specs=[pl.BlockSpec(memory_space=pltpu.SMEM), whole, whole],
        out_specs=pl.BlockSpec(memory_space=pltpu.HBM),
        out_shape=jax.ShapeDtypeStruct((slab, local_cols, width), jnp.bfloat16),
        scratch_shapes=[
            pltpu.VMEM((chunks, lanes // chunks, width), jnp.float32),
            pltpu.VMEM((slab, local_cols, width), jnp.bfloat16),
            pltpu.SemaphoreType.DMA((chunks,)),
        ],
        compiler_params=pltpu.CompilerParams(vmem_limit_bytes=48 * 2**20),
        name="last_contract",
    )(turn, sent, virt_rows)


def rows_kernel(core_ref, blocks_ref, table_ref, own_ref, other_ref, out_ref, full_ref, kept_ref):
    kept_ref[...] = widened(table_ref[1], own_ref.shape[1])
    core = core_ref[0]
    for panel in range(own_ref.shape[0] // PANEL):
        here = pl.ds(panel * PANEL, PANEL)
        for ref, place in ((own_ref, core), (other_ref, 1 - core)):
            first = pl.multiple_of((2 * panel + place) * PANEL, PANEL)
            full_ref[pl.ds(first, PANEL), :] = ref[here, :].astype(jnp.float32)
    count, size, _ = out_ref.shape
    for block in range(count):
        first = pl.multiple_of(blocks_ref[block] * size, SUB)
        kept = kept_ref[pl.ds(blocks_ref[block], 1), :]
        out_ref[block] = (full_ref[pl.ds(first, size), :] * kept).astype(jnp.bfloat16)


def block_rows(core, blocks, green_mask, own, other, size):
    whole = pl.BlockSpec(memory_space=pltpu.VMEM)
    scalars = pl.BlockSpec(memory_space=pltpu.SMEM)
    depth, width = 2 * own.shape[0], own.shape[1]
    return pl.pallas_call(
        rows_kernel,
        in_specs=[scalars, scalars, whole, whole, whole],
        out_specs=whole,
        out_shape=jax.ShapeDtypeStruct((depth // size, size, width), jnp.bfloat16),
        scratch_shapes=[
            pltpu.VMEM((depth, width), jnp.float32),
            pltpu.VMEM((green_mask.shape[1], width), jnp.float32),
        ],
        compiler_params=pltpu.CompilerParams(vmem_limit_bytes=32 * 2**20),
        name="block_rows",
    )(core, blocks, green_mask, own, other)


def shards(three_centre, x_mask, occ_green, virt_green, green_mask, nu_blocks):
    nu_local, slab, width = three_centre.shape
    block_count = green_mask.shape[1]
    block_size = width // block_count
    groups = lax.axis_size("ri")
    members = lax.axis_size("ao")
    place = lax.axis_index("ao").astype(jnp.int32)
    core = (place % 2)[None]
    same_core = [[z * 2 + c for z in range(members // 2)] for c in range(2)]
    both_cores = [(a, a ^ 1) for a in range(members)]

    def gather(panel):
        return lax.all_gather(panel, "ao", axis=0, tiled=True, axis_index_groups=same_core)

    def swap(half):
        return lax.ppermute(half, "ao", both_cores)

    own, after = lax.optimization_barrier((gather(occ_green), core))
    tensor, kept, table = lax.optimization_barrier((fetch(after, three_centre), x_mask, green_mask))
    blank = jnp.zeros((-kept.shape[1] % SUB, block_count), jnp.float32)
    table = jnp.concatenate([table[0].astype(jnp.float32), kept[0].astype(jnp.float32), blank], 0)
    outgoing = half_contract(core, tensor, table, own, swap(own), groups)
    outgoing, virt_panel = lax.optimization_barrier((outgoing, virt_green))
    sent = lax.all_to_all(outgoing, "ri", split_axis=0, concat_axis=0, tiled=True)
    own = gather(virt_panel)
    virt_rows = block_rows(core, nu_blocks, green_mask, own, swap(own), block_size).reshape(width, width)
    turn = (lax.axis_index("ri") * (width // groups // SUB) % GROUP).astype(jnp.int32)[None]
    return last_contract(sent.reshape(width, -1), virt_rows, turn, slab, width // groups)


def solution(mesh):
    return jax.shard_map(
        shards,
        mesh=mesh,
        in_specs=(P("ri", "ao", None), P("ri", "ao", None), P("ao", None), P("ao", None), P(), P()),
        out_specs=P("ao", "ri", None),
        check_vma=False,
    )
```

```python
import functools

import jax
import jax.numpy as jnp
from jax import lax
from jax.experimental import pallas as pl
from jax.experimental.pallas import tpu as pltpu
from jax.sharding import PartitionSpec as P

LANES = 128
SUB = 8
GROUP = LANES // SUB
PANEL = 32
PIECE = 6


def exchange(parts):
    shape = parts[0].shape
    lane_group = lax.broadcasted_iota(jnp.int32, shape, 1) // SUB
    now = [pltpu.roll(part, SUB * p, 1) if p else part for p, part in enumerate(parts)]
    now = [now[(-k) % GROUP] for k in range(GROUP)]
    for bit in (1, 2, 4, 8):
        taken = (lane_group & bit) != 0
        now = [jnp.where(taken, now[(k - bit) % GROUP], now[k]) for k in range(GROUP)]
    return now


def widened(table, width):
    count = table.shape[1]
    size = width // count
    column = lax.broadcasted_iota(jnp.int32, (count, width), 1)
    first = lax.broadcasted_iota(jnp.int32, (count, width), 0) * size
    spread = ((column >= first) & (column < first + size)).astype(jnp.float32).astype(jnp.bfloat16)
    table = table.astype(jnp.float32).astype(jnp.bfloat16)
    return jnp.dot(table, spread, preferred_element_type=jnp.float32)


def fetch_kernel(core_ref, x_hbm, out_ref, sems):
    del core_ref
    pieces = [pl.ds(first, PIECE) for first in range(0, out_ref.shape[0], PIECE)]
    copies = [pltpu.make_async_copy(x_hbm.at[r], out_ref.at[r], sems.at[i]) for i, r in enumerate(pieces)]
    for copy in copies:
        copy.start()
    for copy in copies:
        copy.wait()


def half_kernel(core_ref, table_ref, own_ref, other_ref, x_ref, out_hbm, keep_ref, occ_ref, half_ref, out_ref, out_sems):
    rows, ri_rows, width = x_ref.shape
    slab = GROUP
    chunks = ri_rows // slab
    groups = out_hbm.shape[0]
    size = width // groups

    first_core = core_ref[0] == 0

    def place(columns):
        for panel in range(width // PANEL):
            here = pl.ds(panel // 2 * PANEL, PANEL)
            pair = (own_ref[here, columns], other_ref[here, columns])
            rows_of = lax.select(first_core, pair[panel % 2], pair[1 - panel % 2])
            blocks = [(panel * PANEL + row) // size for row in range(0, PANEL, SUB)]
            kept = [jnp.broadcast_to(keep_ref[i : i + 1, columns], (SUB, span)) for i in blocks]
            there = pl.ds(panel * PANEL, PANEL)
            occ_ref[there, columns] = rows_of * jnp.concatenate(kept, 0).astype(jnp.bfloat16)

    keep_ref[...] = widened(table_ref[...], width)
    span = 2 * LANES
    spans = width // span
    thirds = size // SUB
    lanes = thirds * LANES

    def masked(c):
        blocks = [groups + c * slab // SUB + i for i in range(slab // SUB)]
        kept = jnp.concatenate([jnp.broadcast_to(keep_ref[i : i + 1, :], (SUB, width)) for i in blocks], 0)
        return (x_ref[:, c * slab : (c + 1) * slab, :] * kept.astype(jnp.bfloat16)[None]).reshape(rows * slab, width)

    def multiply(step, tensor):
        first = step % spans * span
        half = jnp.dot(tensor, occ_ref[:, first : first + span], preferred_element_type=jnp.float32)
        for part in range(span // LANES):
            half_ref[step % 2, part] = half[:, part * LANES : (part + 1) * LANES]

    def regroup(step):
        for part in range(span // LANES):
            plane = step % spans * (span // LANES) + part
            part_ref = half_ref.at[step % 2, part]
            parts = [part_ref[pl.ds(p, rows, stride=slab), :] for p in range(slab)]
            for low, piece in enumerate(exchange(parts)):
                group, third = divmod(plane * GROUP + low, thirds)
                first = step // spans * lanes + third * LANES
                out_ref[group, :, first : first + LANES] = piece.astype(jnp.bfloat16)

    out_copies = []
    for step in range(chunks * spans + 1):
        if step < chunks * spans:
            if step % spans == 0:
                tensor = masked(step // spans)
            if step < spans:
                place(pl.ds(step * span, span))
            multiply(step, tensor)
        if step:
            regroup(step - 1)
        if step and step % spans == 0:
            these = pl.ds((step // spans - 1) * lanes, lanes)
            copy = pltpu.make_async_copy(
                out_ref.at[:, :, these], out_hbm.at[:, :, these], out_sems.at[step // spans - 1]
            )
            copy.start()
            out_copies.append(copy)
    for copy in out_copies:
        copy.wait()


def last_kernel(turn_ref, sent_ref, virt_ref, out_hbm, sum_ref, done_ref, sems):
    slab, local_cols, width = out_hbm.shape
    chunks = slab // GROUP
    part = sent_ref.shape[1] // chunks
    turn = turn_ref[0]

    def multiply(c):
        sum_ref[c] = lax.dot_general(
            sent_ref[:, c * part : (c + 1) * part],
            virt_ref[...],
            (((0,), (0,)), ((), ())),
            preferred_element_type=jnp.float32,
        )

    copies = []
    multiply(0)
    for c in range(chunks):
        if c + 1 < chunks:
            multiply(c + 1)
        for p in range(GROUP):
            pieces = [
                sum_ref[c, pl.ds(pl.multiple_of(third * LANES + lax.rem(p + turn + third, GROUP) * SUB, SUB), SUB), :]
                for third in range(local_cols // SUB)
            ]
            done_ref[c * GROUP + p] = jnp.concatenate(pieces, 0).astype(jnp.bfloat16)
        these = pl.ds(c * GROUP, GROUP)
        copies.append(pltpu.make_async_copy(done_ref.at[these], out_hbm.at[these], sems.at[c]))
        copies[-1].start()
    for copy in copies:
        copy.wait()


def fetch(core, three_centre):
    return pl.pallas_call(
        fetch_kernel,
        in_specs=[pl.BlockSpec(memory_space=pltpu.SMEM), pl.BlockSpec(memory_space=pltpu.HBM)],
        out_specs=pl.BlockSpec(memory_space=pltpu.VMEM),
        out_shape=jax.ShapeDtypeStruct(three_centre.shape, jnp.bfloat16),
        scratch_shapes=[pltpu.SemaphoreType.DMA((three_centre.shape[0] // PIECE,))],
        compiler_params=pltpu.CompilerParams(vmem_limit_bytes=51 * 2**20),
        name="fetch",
    )(core, three_centre)


def half_contract(core, three_centre, table, own, other, groups):
    rows, slab, width = three_centre.shape
    chunks = slab // GROUP
    lanes = width // groups * GROUP
    whole = pl.BlockSpec(memory_space=pltpu.VMEM)
    return pl.pallas_call(
        half_kernel,
        in_specs=[
            pl.BlockSpec(memory_space=pltpu.SMEM),
            whole,
            whole,
            whole,
            whole,
        ],
        out_specs=pl.BlockSpec(memory_space=pltpu.HBM),
        out_shape=jax.ShapeDtypeStruct((groups, rows, chunks * lanes), jnp.bfloat16),
        scratch_shapes=[
            pltpu.VMEM((table.shape[0], width), jnp.float32),
            pltpu.VMEM((width, width), jnp.bfloat16),
            pltpu.VMEM((2, 2, rows * GROUP, LANES), jnp.float32),
            pltpu.VMEM((groups, rows, chunks * lanes), jnp.bfloat16),
            pltpu.SemaphoreType.DMA((chunks,)),
        ],
        compiler_params=pltpu.CompilerParams(vmem_limit_bytes=32 * 2**20),
        name="half_contract",
    )(core, table, own, other, three_centre)


def last_contract(sent, virt_rows, turn, slab, local_cols):
    lanes = sent.shape[1]
    width = virt_rows.shape[1]
    chunks = slab // GROUP
    whole = pl.BlockSpec(memory_space=pltpu.VMEM)
    return pl.pallas_call(
        last_kernel,
        in_specs=[pl.BlockSpec(memory_space=pltpu.SMEM), whole, whole],
        out_specs=pl.BlockSpec(memory_space=pltpu.HBM),
        out_shape=jax.ShapeDtypeStruct((slab, local_cols, width), jnp.bfloat16),
        scratch_shapes=[
            pltpu.VMEM((chunks, lanes // chunks, width), jnp.float32),
            pltpu.VMEM((slab, local_cols, width), jnp.bfloat16),
            pltpu.SemaphoreType.DMA((chunks,)),
        ],
        compiler_params=pltpu.CompilerParams(vmem_limit_bytes=48 * 2**20),
        name="last_contract",
    )(turn, sent, virt_rows)


def rows_kernel(core_ref, blocks_ref, table_ref, own_ref, other_ref, out_ref, full_ref, kept_ref):
    kept_ref[...] = widened(table_ref[1], own_ref.shape[1])
    core = core_ref[0]
    for panel in range(own_ref.shape[0] // PANEL):
        here = pl.ds(panel * PANEL, PANEL)
        for ref, place in ((own_ref, core), (other_ref, 1 - core)):
            first = pl.multiple_of((2 * panel + place) * PANEL, PANEL)
            full_ref[pl.ds(first, PANEL), :] = ref[here, :].astype(jnp.float32)
    count, size, _ = out_ref.shape
    for block in range(count):
        first = pl.multiple_of(blocks_ref[block] * size, SUB)
        kept = kept_ref[pl.ds(blocks_ref[block], 1), :]
        out_ref[block] = (full_ref[pl.ds(first, size), :] * kept).astype(jnp.bfloat16)


def block_rows(core, blocks, green_mask, own, other, size):
    whole = pl.BlockSpec(memory_space=pltpu.VMEM)
    scalars = pl.BlockSpec(memory_space=pltpu.SMEM)
    depth, width = 2 * own.shape[0], own.shape[1]
    return pl.pallas_call(
        rows_kernel,
        in_specs=[scalars, scalars, whole, whole, whole],
        out_specs=whole,
        out_shape=jax.ShapeDtypeStruct((depth // size, size, width), jnp.bfloat16),
        scratch_shapes=[
            pltpu.VMEM((depth, width), jnp.float32),
            pltpu.VMEM((green_mask.shape[1], width), jnp.float32),
        ],
        compiler_params=pltpu.CompilerParams(vmem_limit_bytes=32 * 2**20),
        name="block_rows",
    )(core, blocks, green_mask, own, other)


def shards(three_centre, x_mask, occ_green, virt_green, green_mask, nu_blocks):
    nu_local, slab, width = three_centre.shape
    block_count = green_mask.shape[1]
    block_size = width // block_count
    groups = lax.axis_size("ri")
    members = lax.axis_size("ao")
    place = lax.axis_index("ao").astype(jnp.int32)
    core = (place % 2)[None]
    same_core = [[z * 2 + c for z in range(members // 2)] for c in range(2)]
    both_cores = [(a, a ^ 1) for a in range(members)]

    def gather(panel):
        return lax.all_gather(panel, "ao", axis=0, tiled=True, axis_index_groups=same_core)

    def swap(half):
        return lax.ppermute(half, "ao", both_cores)

    own, after = lax.optimization_barrier((gather(occ_green), core))
    tensor, kept, table = lax.optimization_barrier((fetch(after, three_centre), x_mask, green_mask))
    blank = jnp.zeros((-kept.shape[1] % SUB, block_count), jnp.float32)
    table = jnp.concatenate([table[0].astype(jnp.float32), kept[0].astype(jnp.float32), blank], 0)
    outgoing = half_contract(core, tensor, table, own, swap(own), groups)
    outgoing, virt_panel = lax.optimization_barrier((outgoing, virt_green))
    sent = lax.all_to_all(outgoing, "ri", split_axis=0, concat_axis=0, tiled=True)
    own = gather(virt_panel)
    virt_rows = block_rows(core, nu_blocks, green_mask, own, swap(own), block_size).reshape(width, width)
    turn = (lax.axis_index("ri") * (width // groups // SUB) % GROUP).astype(jnp.int32)[None]
    return last_contract(sent.reshape(width, -1), virt_rows, turn, slab, width // groups)


def solution(mesh):
    return jax.shard_map(
        shards,
        mesh=mesh,
        in_specs=(P("ri", "ao", None), P("ri", "ao", None), P("ao", None), P("ao", None), P(), P()),
        out_specs=P("ao", "ri", None),
        check_vma=False,
    )
```
